32 devices in a mesh: site: 16 (over z, y, x), batch: 2 (over core).
Axes of the slice: x: 2, y: 2, z: 4, core: 2. Of those that a mesh axis runs over, the one named last changes fastest.
Arguments:
- site_tensors: bfloat16 [16, 2, 32, 128, 128], P('site')
- start_vector: float32 [16, 128], P('batch'), may hold values from -6 to 6
- start_label: int32 [16], P('batch'), may hold values from 0 to 31
- occupations: int32 [16, 16], P('site', 'batch'), may hold values from 0 to 1
Outputs:
- fill_prob: float32 [16, 16], P('site', 'batch')
- mean_logprob: float32 [16], P('batch')
- site_fill: float32 [16], P('site')
The draws below stay inside these ranges and needn't reach their ends.
All inputs are finite; a program needn't handle non-finite values.
Results may differ from the reference program's by a relative error of at most 0.0003.
Values sent between devices are 32-bit elements; how exact they have to be, the bound alone decides.
No kernel may reach another device: no remote copies, remote signals or barrier semaphores. Data moves between devices by JAX's collectives and lax.ppermute only.
A program may use at most 128 MiB of HBM per device.

```python
import math
import jax
import jax.numpy as jnp
from jax import lax

BLOCK = 128
SECTORS = 32
SITES = 16
SAMPLES = 16


def draw_site_tensors(key, part):
    width = BLOCK
    lead = (2, SECTORS)

    def one_site(site_number):
        site_key = jax.random.fold_in(key, site_number)
        row_scores = jax.random.randint(jax.random.fold_in(site_key, 11), lead + (width,), 0, 1 << 20) * width + jnp.arange(width, dtype=jnp.int32)
        col_scores = jax.random.randint(jax.random.fold_in(site_key, 12), lead + (width,), 0, 1 << 20) * width + jnp.arange(width, dtype=jnp.int32)
        row_perm = jnp.argsort(row_scores, axis=-1).astype(jnp.int32)
        col_perm = jnp.argsort(col_scores, axis=-1).astype(jnp.int32)
        signs = (2 * jax.random.randint(jax.random.fold_in(site_key, 13), lead + (width,), 0, 2) - 1).astype(jnp.float32)
        freq = row_perm[..., :, None]
        spot = col_perm[..., None, :]
        phase = (2 * spot + 1) * freq % (4 * width)
        angle = phase.astype(jnp.float32) * (math.pi / (2.0 * width))
        norm_row = jnp.where(freq == 0, math.sqrt(1.0 / width), math.sqrt(2.0 / width)).astype(jnp.float32)
        ortho = signs[..., :, None] * norm_row * jnp.cos(angle)
        noise_key = jax.random.fold_in(site_key, 14)
        noise = jax.random.truncated_normal(noise_key, -4.0, 4.0, lead + (width, width), jnp.float32)
        low_gain = math.log(0.8)
        high_gain = math.log(1.25)
        noise = noise * (0.15 / math.sqrt(width))
        levels = jax.random.uniform(jax.random.fold_in(site_key, 15), lead + (1, width), jnp.float32, -math.sqrt(3.0), math.sqrt(3.0))
        column_scale = jnp.exp(0.2 * levels)
        gains = jnp.exp(jax.random.uniform(jax.random.fold_in(site_key, 16), lead + (1, 1), jnp.float32, low_gain, high_gain))
        return (gains * (ortho + noise) * column_scale).astype(jnp.float32)
    whole = lax.map(one_site, jnp.arange(SITES, dtype=jnp.int32))
    return whole.astype(jnp.bfloat16)


def touch_ends(values, stream_key, least, high):
    shape = values.shape
    place = [jax.random.randint(jax.random.fold_in(stream_key, axis), (), 0, shape[axis]) for axis in range(len(shape))]
    values = values.at[tuple(place)].set(least)
    longest = shape.index(max(shape))
    place[longest] = (place[longest] + 1) % shape[longest]
    return values.at[tuple(place)].set(high)


def block_scale(key, shape, pieces, low, top_value):
    loudness = 1.0
    for axis_at, parts in pieces:
        steps = jax.random.uniform(jax.random.fold_in(jax.random.fold_in(key, 6), axis_at), (parts,), jnp.float32, low / len(pieces), top_value / len(pieces))
        loudness = loudness * jnp.repeat(jnp.exp(steps), shape[axis_at] // parts).reshape((-1,) + (1,) * (len(shape) - 1 - axis_at))
    return loudness


def bell_draw(key, extent, spread, limit, split=(), kind=jnp.bfloat16):
    factor_of = block_scale(key, extent, split, -0.22, 0.18) if split else 1.0
    values = jax.random.normal(key, extent, jnp.float32) * spread * factor_of
    return jnp.minimum(jnp.maximum(values, -limit), limit).astype(kind)


def setup_inputs(seed: int = 0) -> dict:
    key_list = jax.random.split(jax.random.key(seed), 5)
    site_tensors = draw_site_tensors(jax.random.fold_in(key_list[4], 71), 0)
    start_vector = bell_draw(key_list[1], (SAMPLES, BLOCK), 1.0, 6.0, ((0, 2),), jnp.float32)
    start_label = touch_ends(jax.random.randint(key_list[2], (SAMPLES,), 0, SECTORS), jax.random.fold_in(key_list[2], 1), 0, SECTORS - 1).astype(jnp.int32)
    occupations = touch_ends(jax.random.randint(key_list[3], (SITES, SAMPLES), 0, 2), jax.random.fold_in(key_list[3], 1), 0, 1).astype(jnp.int32)
    return dict(site_tensors=site_tensors, start_vector=start_vector, start_label=start_label, occupations=occupations)


epsilon = 1e-6


def reference(site_tensors, start_vector, start_label, occupations):
    flat_tensors = site_tensors.reshape(SITES, 2 * SECTORS, BLOCK, BLOCK)

    def advance(state_pair, inputs):
        vector, sector_label = state_pair
        block_table, occupied = inputs
        zero_blocks = jnp.take(block_table, sector_label, axis=0).astype(jnp.float32)
        one_blocks = jnp.take(block_table, sector_label + SECTORS, axis=0).astype(jnp.float32)
        w_zero = jnp.einsum("sa,sab->sb", vector, zero_blocks, precision=lax.Precision.HIGHEST)
        w_one = jnp.einsum("sa,sab->sb", vector, one_blocks, precision=lax.Precision.HIGHEST)
        e_zero = jnp.sum(w_zero * w_zero, axis=1)
        e_one = jnp.sum(w_one * w_one, axis=1)
        total = e_zero + e_one + epsilon
        fill_probs = e_one / total
        chosen = jnp.where(occupied == 1, e_one, e_zero)
        log_term = jnp.log(chosen + epsilon) - jnp.log(total)
        vector = jnp.where((occupied == 1)[:, None], w_one, w_zero)
        sector_label = ((sector_label + occupied) % SECTORS).astype(jnp.int32)
        return (vector, sector_label), (fill_probs, log_term)

    state_start = (start_vector.astype(jnp.float32), start_label.astype(jnp.int32))
    finals, outputs = lax.scan(advance, state_start, (flat_tensors, occupations.astype(jnp.int32)))
    fill_prob, log_terms = outputs
    mean_logprob = jnp.sum(log_terms, axis=0) / SITES
    site_fill = jnp.sum(fill_prob, axis=1) / SAMPLES
    return fill_prob, mean_logprob, site_fill
```

```python
import functools

import jax
import jax.numpy as jnp
from jax import lax
from jax.experimental import pallas as pl
from jax.experimental.pallas import tpu as pltpu
from jax.sharding import PartitionSpec as P

epsilon = 1e-06
LANES = 128


def fetch_kernel(picks, table, out, held, sems):
    samples = out.shape[0]
    copies = [
        pltpu.make_async_copy(table.at[picks[n, s]], held.at[s, n], sems.at[s, n])
        for s in range(samples)
        for n in range(2)
    ]
    for copy in copies:
        copy.start()
    at = 0
    for s in range(samples):
        for n in range(2):
            copies[at].wait()
            at += 1
            out[s, n] = held[s, n].astype(jnp.float32)


def fetch_blocks(picks, table):
    samples = picks.shape[1]
    width = table.shape[-1]
    shape = (samples, 2, width, width)
    return pl.pallas_call(
        fetch_kernel,
        grid_spec=pltpu.PrefetchScalarGridSpec(
            num_scalar_prefetch=1,
            grid=(1,),
            in_specs=[pl.BlockSpec(memory_space=pl.ANY)],
            out_specs=pl.BlockSpec(shape, lambda i, picks: (0, 0, 0, 0)),
            scratch_shapes=[
                pltpu.VMEM(shape, table.dtype),
                pltpu.SemaphoreType.DMA((samples, 2)),
            ],
        ),
        out_shape=jax.ShapeDtypeStruct(shape, jnp.float32),
        compiler_params=pltpu.CompilerParams(vmem_limit_bytes=16 << 20),
        name="fetch_blocks",
    )(picks, table)


def halves(x):
    high = x.astype(jnp.bfloat16)
    low = (x - high.astype(jnp.float32)).astype(jnp.bfloat16)
    return high, low


def times_block(left, block):
    high, low = halves(left)
    rows = left.shape[0]
    both = jnp.dot(
        jnp.concatenate([high, low], axis=0), block, preferred_element_type=jnp.float32
    )
    return both[:rows] + both[rows:]


def as_column(row):
    width = row.shape[-1]
    return jnp.broadcast_to(row, (width, width)).T


def products_kernel(blocks, start, out, leaving):
    steps = blocks.shape[0]
    left = None
    for k in range(steps):
        chosen = blocks[k, 0]
        other = blocks[k, 1]
        if left is None:
            out[0, 1] = other
            left = chosen
        else:
            out[k, 1] = times_block(left, other.astype(jnp.bfloat16))
            left = times_block(left, chosen.astype(jnp.bfloat16))
        out[k, 0] = left
    leaving[...] = jnp.sum(as_column(start[0:1, :]) * left, axis=0, keepdims=True)


def group_products(blocks, start):
    whole = pl.BlockSpec(memory_space=pltpu.VMEM)
    return pl.pallas_call(
        products_kernel,
        in_specs=[whole, whole],
        out_specs=[whole, whole],
        out_shape=[
            jax.ShapeDtypeStruct(blocks.shape, jnp.float32),
            jax.ShapeDtypeStruct((1, blocks.shape[-1]), jnp.float32),
        ],
        compiler_params=pltpu.CompilerParams(vmem_limit_bytes=16 << 20),
        name="group_products",
    )(blocks, start)


def weights_kernel(products, vector, out):
    steps = products.shape[0]
    column = as_column(vector[...])
    for k in range(steps):
        for n in range(2):
            row = jnp.sum(column * products[k, n], axis=0, keepdims=True)
            total = jnp.sum(row * row, axis=1, keepdims=True)
            out[n, k : k + 1, :] = jnp.broadcast_to(total, (1, LANES))


def group_weights(products, vector):
    whole = pl.BlockSpec(memory_space=pltpu.VMEM)
    return pl.pallas_call(
        weights_kernel,
        in_specs=[whole, whole],
        out_specs=whole,
        out_shape=jax.ShapeDtypeStruct((2, products.shape[0], LANES), jnp.float32),
        compiler_params=pltpu.CompilerParams(vmem_limit_bytes=16 << 20),
        name="group_weights",
    )(products, vector)


def on_device(site_tensors, start_vector, start_label, occupations):
    sectors = site_tensors.shape[2]
    width = site_tensors.shape[3]
    sites = lax.axis_size("site")
    batches = lax.axis_size("batch")
    samples = occupations.shape[1]
    group = samples
    groups = sites // group
    everyone = sites * batches
    place = lax.axis_index("site")
    batch = lax.axis_index("batch")
    mine = place % group
    here = place // group

    table = site_tensors.reshape(2 * sectors, width, width)
    occupied = occupations[0]

    row = jnp.pad(occupied, (0, LANES - samples))[None, :]
    heard = lax.all_to_all(
        jnp.broadcast_to(row, (everyone, LANES)), ("site", "batch"), 0, 0, tiled=True
    )
    heard = heard.reshape(sites, batches, LANES)
    all_occupied = lax.dynamic_index_in_dim(heard, batch, 1, False)[:, :samples]
    before = (jnp.arange(sites) < place)[:, None]
    earlier = jnp.sum(jnp.where(before, all_occupied, 0), axis=0)
    label = (start_label + earlier) % sectors
    picks = jnp.stack([label + sectors * occupied, label + sectors * (1 - occupied)])

    blocks = fetch_blocks(picks, table)
    teams = [[g * group + k for k in range(group)] for g in range(groups)]
    blocks = lax.all_to_all(blocks, "site", 0, 0, tiled=True, axis_index_groups=teams)

    start = lax.dynamic_slice_in_dim(start_vector, mine, 1, 0)
    products, leaving = group_products(blocks, start)

    vector = start
    onward = [(i, (i + group) % sites) for i in range(sites)]
    for turn in range(1, groups):
        if turn > 1:
            leaving = jnp.einsum(
                "sa,ab->sb", vector, products[-1, 0], precision=lax.Precision.HIGHEST
            )
        arrived = lax.ppermute(leaving, "site", onward)
        vector = jnp.where(here == turn, arrived, vector)

    found = group_weights(products, vector)[:, :, 0]
    of_chosen, of_other = found[0], found[1]
    group_occupied = lax.dynamic_slice(all_occupied, (here * group, mine), (group, 1))[:, 0]
    e_one = jnp.where(group_occupied == 1, of_chosen, of_other)
    total = of_chosen + of_other + epsilon
    fill = e_one / total
    log_sum = jnp.sum(jnp.log(of_chosen + epsilon) - jnp.log(total))

    fill_of_site = jnp.zeros((groups, group), jnp.float32)
    fill_of_site = jnp.where((jnp.arange(groups) == here)[:, None], fill[None, :], 0.0)
    fill_of_site = jnp.repeat(fill_of_site.reshape(sites), batches)
    lane = jnp.arange(LANES)[None, :]
    message = jnp.where(
        lane == 0, fill_of_site[:, None], jnp.where(lane == 1, log_sum, 0.0)
    ).astype(jnp.float32)
    reply = lax.all_to_all(message, ("site", "batch"), 0, 0, tiled=True)
    reply = reply.reshape(groups, group, batches, LANES)
    own = lax.dynamic_index_in_dim(reply, batch, 2, False)
    fill_probs = jnp.sum(own[:, :, 0], axis=0)
    mean_logprob = jnp.sum(own[:, :, 1], axis=0) / sites
    site_fill = jnp.sum(reply[:, :, :, 0])[None] / (samples * batches)
    return (fill_probs[None, :], mean_logprob, site_fill)


def solution(mesh):
    placed = (P("site", None, None, None, None), P("batch", None), P("batch"), P("site", "batch"))
    return jax.shard_map(
        on_device,
        mesh=mesh,
        in_specs=placed,
        out_specs=(P("site", "batch"), P("batch"), P("site")),
        check_vma=False,
    )
```

```python
import jax
import jax.numpy as jnp
from jax import lax
from jax.experimental import pallas as pl
from jax.experimental.pallas import tpu as pltpu
from jax.sharding import PartitionSpec as P

epsilon = 1e-06
LANES = 128
VMEM_BYTES = 24 << 20


def whole():
    return pl.BlockSpec(memory_space=pltpu.VMEM)


def lanes_of(shape):
    return lax.broadcasted_iota(jnp.int32, shape, 1)


def rows_of(shape):
    return lax.broadcasted_iota(jnp.int32, shape, 0)


def tell_kernel(sites, group, occupied, out, row):
    place, batch = lax.axis_index("site"), lax.axis_index("batch")
    samples = occupied.shape[1]
    row[...] = jnp.zeros_like(row)
    row[0:1, 0:samples] = occupied[...]
    shape = out.shape
    occ = row[0:1, :]
    lane = lanes_of(shape)
    to = rows_of(shape)
    to_batch, to_site = to // sites, to % sites
    later = jnp.where(to_site > place, occ, 0)
    owned = jnp.sum(jnp.where(lane == to_site % group, occ, 0), axis=1, keepdims=True)
    message = jnp.where(lane < samples, later, jnp.where(lane == samples, owned, 0))
    out[...] = jnp.where(to_batch == batch, message, 0)


def keep_kernel(table, out, sem):
    copy = pltpu.make_async_copy(table, out, sem)
    copy.start()
    copy.wait()


def keep(table):
    return pl.pallas_call(
        keep_kernel,
        in_specs=[pl.BlockSpec(memory_space=pltpu.HBM)],
        out_specs=whole(),
        scratch_shapes=[pltpu.SemaphoreType.DMA],
        out_shape=jax.ShapeDtypeStruct(table.shape, table.dtype),
        compiler_params=pltpu.CompilerParams(vmem_limit_bytes=VMEM_BYTES),
        cost_estimate=pl.CostEstimate(flops=0, bytes_accessed=4 * table.size, transcendentals=0),
        name="keep",
    )(table)


def fetch_kernel(sectors, heard, occupied, start_label, table, out, row):
    samples = out.shape[0]
    row[...] = jnp.zeros_like(row)
    row[0:1, 0:samples] = start_label[...]
    row[1:2, 0:samples] = occupied[...] * sectors
    label = (jnp.sum(heard[...], axis=0, keepdims=True) + row[0:1, :]) % sectors
    chosen = label + row[1:2, :]
    other = label + sectors - row[1:2, :]
    for s in range(samples):
        out[s, 0] = table[chosen[0, s]].astype(jnp.float32)
        out[s, 1] = table[other[0, s]].astype(jnp.float32)


def times_block(left, block):
    high = left.astype(jnp.bfloat16)
    low = (left - high.astype(jnp.float32)).astype(jnp.bfloat16)
    rows = left.shape[0]
    both = jnp.dot(
        jnp.concatenate([high, low], axis=0), block, preferred_element_type=jnp.float32
    )
    return both[:rows] + both[rows:]


def as_column(row):
    width = row.shape[-1]
    return jnp.broadcast_to(row, (width, width)).T


def products_kernel(group, blocks, start, products, leaving, own_start):
    mine = lax.axis_index("site") % group
    vector = start[pl.ds(mine, 1), :]
    own_start[...] = vector
    left = blocks[0, 0]
    products[0] = left
    for k in range(1, group):
        left = times_block(left, blocks[k, 0].astype(jnp.bfloat16))
        products[k] = left
    leaving[...] = jnp.sum(as_column(vector) * left, axis=0, keepdims=True)


def weights_kernel(sites, group, products, blocks, own_start, arrived, heard, out):
    place, batch = lax.axis_index("site"), lax.axis_index("batch")
    mine, here = place % group, place // group
    groups = sites // group
    vector = jnp.where(here == groups - 1, arrived[...], own_start[...]) if groups > 1 else own_start[...]
    column = as_column(vector)
    rows = [vector]
    for k in range(group):
        rows.append(jnp.sum(column * products[k], axis=0, keepdims=True))
    entering = jnp.concatenate(rows[:group], axis=0)
    after = jnp.concatenate(rows[1:], axis=0)
    columns = entering.T
    beside = []
    for k in range(group):
        column = jnp.broadcast_to(columns[:, k : k + 1], (columns.shape[0],) * 2)
        beside.append(jnp.sum(column * blocks[k, 1], axis=0, keepdims=True))
    beside = jnp.concatenate(beside, axis=0)
    of_chosen = jnp.sum(after * after, axis=1, keepdims=True)
    of_other = jnp.sum(beside * beside, axis=1, keepdims=True)
    notes = heard[pl.ds(pl.multiple_of(batch * sites + here * group, group), group), :]
    occupied = notes[:, group : group + 1]
    total = of_chosen + of_other + epsilon
    fill = jnp.where(occupied == 1, of_chosen, of_other) / total
    log_sum = jnp.sum(jnp.log(of_chosen + epsilon) - jnp.log(total), axis=0, keepdims=True)
    lane = lanes_of((group, LANES))
    fill_own = jnp.where(lane == mine, fill, 0.0)
    fill_cross = jnp.where(lane == 2 * group, fill, 0.0)
    logs = jnp.where(lane == group + mine, log_sum, 0.0)
    for b in range(out.shape[0] // sites):
        for g in range(groups):
            at = b * sites + g * group
            fills = jnp.where(batch == b, fill_own, fill_cross)
            out[at : at + group, :] = jnp.where(here == g, fills, 0.0) + jnp.where(
                batch == b, logs, 0.0
            )


def collect_kernel(sites, batches, reply, fill_probs, mean_logprob, site_fill):
    samples = fill_probs.shape[1]
    row = jnp.sum(reply[...], axis=0, keepdims=True)
    fill_probs[...] = row[:, :samples]
    mean_logprob[...] = row[:, samples : 2 * samples] / sites
    lane = lanes_of(row.shape)
    fills = jnp.where((lane < samples) | (lane == 2 * samples), row, 0.0)
    site_fill[...] = jnp.sum(fills, axis=1, keepdims=True) / (samples * batches)


def call(kernel, out_shape, *arrays, scratch_shapes=(), name=None):
    out_specs = [whole()] * len(out_shape) if isinstance(out_shape, list) else whole()
    return pl.pallas_call(
        kernel,
        in_specs=[whole()] * len(arrays),
        out_specs=out_specs,
        out_shape=out_shape,
        scratch_shapes=scratch_shapes,
        compiler_params=pltpu.CompilerParams(vmem_limit_bytes=VMEM_BYTES),
        name=name,
    )(*arrays)


def on_device(site_tensors, start_vector, start_label, occupations):
    sectors = site_tensors.shape[2]
    width = site_tensors.shape[3]
    sites = lax.axis_size("site")
    batches = lax.axis_size("batch")
    samples = occupations.shape[1]
    group = samples
    groups = sites // group
    everyone = sites * batches
    here = lax.axis_index("site") // group
    f32 = jnp.float32

    table = keep(site_tensors.reshape(2 * sectors, width, width))

    told = call(
        lambda *refs: tell_kernel(sites, group, *refs),
        jax.ShapeDtypeStruct((everyone, LANES), jnp.int32),
        occupations,
        scratch_shapes=[pltpu.VMEM((8, LANES), jnp.int32)],
        name="tell",
    )
    heard = lax.all_to_all(told, ("batch", "site"), 0, 0, tiled=True)

    teams = [[g * group + k for k in range(group)] for g in range(groups)]

    blocks = call(
        lambda *refs: fetch_kernel(sectors, *refs),
        jax.ShapeDtypeStruct((samples, 2, width, width), f32),
        heard,
        occupations,
        start_label[None, :],
        table,
        scratch_shapes=[pltpu.VMEM((8, LANES), jnp.int32)],
        name="fetch",
    )
    blocks = lax.all_to_all(blocks, "site", 0, 0, tiled=True, axis_index_groups=teams)

    row = jax.ShapeDtypeStruct((1, width), f32)
    products, leaving, vector = call(
        lambda *refs: products_kernel(group, *refs),
        [jax.ShapeDtypeStruct((group, width, width), f32), row, row],
        blocks,
        start_vector,
        name="group_products",
    )

    onward = [(i, (i + group) % sites) for i in range(sites)]
    arrived = vector
    for turn in range(1, groups):
        if turn > 1:
            vector = jnp.where(here == turn - 1, arrived, vector)
            leaving = jnp.einsum("sa,ab->sb", vector, products[-1], precision=lax.Precision.HIGHEST)
        arrived = lax.ppermute(leaving, "site", onward)

    message = call(
        lambda *refs: weights_kernel(sites, group, *refs),
        jax.ShapeDtypeStruct((everyone, LANES), f32),
        products,
        blocks,
        vector,
        arrived,
        heard,
        name="group_weights",
    )
    reply = lax.all_to_all(message, ("batch", "site"), 0, 0, tiled=True)
    fill_probs, mean_logprob, site_fill = call(
        lambda *refs: collect_kernel(sites, batches, *refs),
        [
            jax.ShapeDtypeStruct((1, samples), f32),
            jax.ShapeDtypeStruct((1, samples), f32),
            jax.ShapeDtypeStruct((1, 1), f32),
        ],
        reply,
        name="collect",
    )
    return (fill_probs, mean_logprob[0], site_fill[0])


def solution(mesh):
    placed = (P("site", None, None, None, None), P("batch", None), P("batch"), P("site", "batch"))
    return jax.shard_map(
        on_device,
        mesh=mesh,
        in_specs=placed,
        out_specs=(P("site", "batch"), P("batch"), P("site")),
        check_vma=False,
    )
```

```python
import jax
import jax.numpy as jnp
from jax import lax
from jax.experimental import pallas as pl
from jax.experimental.pallas import tpu as pltpu
from jax.sharding import PartitionSpec as P

epsilon = 1e-06
LANES = 128
VMEM_BYTES = 24 << 20
LEAD = 9
SEATS = (0, 1, 2, 3, 4, 5, 6, 7)


def whole():
    return pl.BlockSpec(memory_space=pltpu.VMEM)


def lanes_of(shape):
    return lax.broadcasted_iota(jnp.int32, shape, 1)


def rows_of(shape):
    return lax.broadcasted_iota(jnp.int32, shape, 0)


def first_order(sites):
    lead = sites * LEAD // 16
    order = list(range(sites))
    order[0], order[lead] = lead, 0
    return order, lead


def swapped(index, lead):
    return jnp.where(index == 0, lead, jnp.where(index == lead, 0, index))


def keep_kernel(table, out, sem):
    copy = pltpu.make_async_copy(table, out, sem)
    copy.start()
    copy.wait()


def keep(table):
    return pl.pallas_call(
        keep_kernel,
        in_specs=[pl.BlockSpec(memory_space=pltpu.HBM)],
        out_specs=whole(),
        scratch_shapes=[pltpu.SemaphoreType.DMA],
        out_shape=jax.ShapeDtypeStruct(table.shape, table.dtype),
        compiler_params=pltpu.CompilerParams(vmem_limit_bytes=VMEM_BYTES),
        cost_estimate=pl.CostEstimate(flops=0, bytes_accessed=4 * table.size, transcendentals=0),
        name="keep",
    )(table)


def fetch_kernel(sectors, seats, lead, heard, occupied, start_label, table, out):
    place = lax.axis_index("site")
    told = heard[:, 0, :]
    earlier = swapped(rows_of(told.shape), lead) < place
    label = jnp.sum(jnp.where(earlier, told, 0), axis=0, keepdims=True) + start_label[...]
    label = label % sectors
    chosen = label + occupied[...] * sectors
    other = label + sectors - occupied[...] * sectors
    for at, s in enumerate(seats):
        out[at, 0] = table[chosen[0, s]].astype(jnp.float32)
        out[at, 1] = table[other[0, s]].astype(jnp.float32)


def halves(x):
    high = x.astype(jnp.bfloat16)
    return high, (x - high.astype(jnp.float32)).astype(jnp.bfloat16)


def times_exact(left, right):
    rows = left.shape[0]
    both = jnp.dot(
        jnp.concatenate(halves(left), axis=0), right, preferred_element_type=jnp.float32
    )
    return both[:rows] + both[rows:]


def times(left, right):
    high, low = halves(right)
    part = jnp.dot(left.astype(jnp.bfloat16), low, preferred_element_type=jnp.float32)
    return times_exact(left, high) + part


def as_column(row):
    width = row.shape[-1]
    return jnp.broadcast_to(row, (width, width)).T


def leaving_kernel(group, seats, blocks, start, leaving, own_start):
    vector = start[pl.ds(lax.axis_index("site") % group, 1), :]
    own_start[...] = vector
    chosen = [blocks[seats.index(k), 0].astype(jnp.bfloat16) for k in range(group)]
    factors = [
        jnp.dot(chosen[k], chosen[k + 1], preferred_element_type=jnp.float32)
        for k in range(0, group - 1, 2)
    ]
    if group % 2:
        factors.append(chosen[-1].astype(jnp.float32))
    while len(factors) > 2:
        tail = factors[len(factors) // 2 * 2 :]
        factors = [times(factors[k], factors[k + 1]) for k in range(0, len(factors) - 1, 2)] + tail
    for factor in factors:
        vector = jnp.sum(as_column(vector) * factor, axis=0, keepdims=True)
    leaving[...] = vector


def products_kernel(group, seats, blocks, products):
    for k in range(group):
        chosen, other = blocks[seats.index(k), 0], blocks[seats.index(k), 1]
        if k == 0:
            left, beside = chosen, other
        else:
            beside = times_exact(left, other.astype(jnp.bfloat16))
            left = times_exact(left, chosen.astype(jnp.bfloat16))
        products[0, k] = left
        products[1, k] = beside


def weights_kernel(sites, group, lead, products, own_start, arrived, heard, out):
    place, batch = lax.axis_index("site"), lax.axis_index("batch")
    mine, here = place % group, place // group
    groups = sites // group
    vector = own_start[...]
    if groups > 1:
        vector = jnp.where(here == groups - 1, arrived[...], vector)
    column = as_column(vector)

    def weight(n):
        rows = [jnp.sum(column * products[n, k], axis=0, keepdims=True) for k in range(group)]
        rows = jnp.concatenate(rows, axis=0)
        return jnp.sum(rows * rows, axis=1, keepdims=True)

    of_chosen, of_other = weight(0), weight(1)
    notes = jnp.concatenate(
        [heard[swapped(here * group + k, lead)] for k in range(group)], axis=0
    )
    notes = jnp.where(lanes_of(notes.shape) == mine, notes, 0)
    occupied = jnp.sum(notes, axis=1, keepdims=True)
    total = of_chosen + of_other + epsilon
    fill = jnp.where(occupied == 1, of_chosen, of_other) / total
    log_sum = jnp.sum(jnp.log(of_chosen + epsilon) - jnp.log(total), axis=0, keepdims=True)
    lane = lanes_of((group, LANES))
    fill_own = jnp.where(lane == mine, fill, 0.0)
    fill_cross = jnp.where(lane == 2 * group, fill, 0.0)
    logs = jnp.where(lane == group + mine, log_sum, 0.0)
    for b in range(out.shape[0] // sites):
        for g in range(groups):
            at = b * sites + g * group
            fills = jnp.where(batch == b, fill_own, fill_cross)
            out[at : at + group, :] = jnp.where(here == g, fills, 0.0) + jnp.where(
                batch == b, logs, 0.0
            )


def collect_kernel(sites, batches, reply, fill_probs, mean_logprob, site_fill):
    samples = fill_probs.shape[1]
    row = jnp.sum(reply[...], axis=0, keepdims=True)
    fill_probs[...] = row[:, :samples]
    mean_logprob[...] = row[:, samples : 2 * samples] / sites
    lane = lanes_of(row.shape)
    fills = jnp.where((lane < samples) | (lane == 2 * samples), row, 0.0)
    site_fill[...] = jnp.sum(fills, axis=1, keepdims=True) / (samples * batches)


def call(kernel, out_shape, *arrays, scratch_shapes=(), name=None):
    out_specs = [whole()] * len(out_shape) if isinstance(out_shape, list) else whole()
    return pl.pallas_call(
        kernel,
        in_specs=[whole()] * len(arrays),
        out_specs=out_specs,
        out_shape=out_shape,
        scratch_shapes=scratch_shapes,
        compiler_params=pltpu.CompilerParams(vmem_limit_bytes=VMEM_BYTES),
        name=name,
    )(*arrays)


def on_device(site_tensors, start_vector, start_label, occupations):
    sectors = site_tensors.shape[2]
    width = site_tensors.shape[3]
    sites = lax.axis_size("site")
    batches = lax.axis_size("batch")
    samples = occupations.shape[1]
    group = samples
    groups = sites // group
    everyone = sites * batches
    here = lax.axis_index("site") // group
    f32 = jnp.float32

    table = keep(site_tensors.reshape(2 * sectors, width, width))

    order, lead = first_order(sites)
    told = jnp.broadcast_to(occupations[:, None, :], (sites, 1, samples))
    heard = lax.all_to_all(told, "site", 0, 0, tiled=True, axis_index_groups=[order])

    seats = SEATS if group == len(SEATS) else tuple(range(group))
    teams = [[g * group + k for k in seats] for g in range(groups)]

    blocks = call(
        lambda *refs: fetch_kernel(sectors, seats, lead, *refs),
        jax.ShapeDtypeStruct((samples, 2, width, width), f32),
        heard,
        occupations,
        start_label[None, :],
        table,
        name="fetch",
    )
    blocks = lax.all_to_all(blocks, "site", 0, 0, tiled=True, axis_index_groups=teams)

    row = jax.ShapeDtypeStruct((1, width), f32)
    leaving, vector = call(
        lambda *refs: leaving_kernel(group, seats, *refs),
        [row, row],
        blocks,
        start_vector,
        name="leaving",
    )
    products = call(
        lambda *refs: products_kernel(group, seats, *refs),
        jax.ShapeDtypeStruct((2, group, width, width), f32),
        blocks,
        name="products",
    )

    onward = [(i, (i + group) % sites) for i in range(sites)]
    arrived = vector
    for turn in range(1, groups):
        if turn > 1:
            vector = jnp.where(here == turn - 1, arrived, vector)
            leaving = jnp.einsum("sa,ab->sb", vector, products[0, -1], precision=lax.Precision.HIGHEST)
        arrived = lax.ppermute(leaving, "site", onward)

    message = call(
        lambda *refs: weights_kernel(sites, group, lead, *refs),
        jax.ShapeDtypeStruct((everyone, LANES), f32),
        products,
        vector,
        arrived,
        heard,
        name="group_weights",
    )
    reply = lax.all_to_all(message, ("batch", "site"), 0, 0, tiled=True)
    fill_probs, mean_logprob, site_fill = call(
        lambda *refs: collect_kernel(sites, batches, *refs),
        [
            jax.ShapeDtypeStruct((1, samples), f32),
            jax.ShapeDtypeStruct((1, samples), f32),
            jax.ShapeDtypeStruct((1, 1), f32),
        ],
        reply,
        name="collect",
    )
    return (fill_probs, mean_logprob[0], site_fill[0])


def solution(mesh):
    placed = (P("site", None, None, None, None), P("batch", None), P("batch"), P("site", "batch"))
    return jax.shard_map(
        on_device,
        mesh=mesh,
        in_specs=placed,
        out_specs=(P("site", "batch"), P("batch"), P("site")),
        check_vma=False,
    )
```

```python
import jax
import jax.numpy as jnp
from jax import lax
from jax.experimental import pallas as pl
from jax.experimental.pallas import tpu as pltpu
from jax.sharding import PartitionSpec as P

epsilon = 1e-06
LANES = 128
VMEM_BYTES = 24 << 20
LEAD = 9


def whole():
    return pl.BlockSpec(memory_space=pltpu.VMEM)


def lanes_of(shape):
    return lax.broadcasted_iota(jnp.int32, shape, 1)


def rows_of(shape):
    return lax.broadcasted_iota(jnp.int32, shape, 0)


def first_order(sites):
    lead = sites * LEAD // 16
    order = list(range(sites))
    order[0], order[lead] = lead, 0
    return order, lead


def swapped(index, lead):
    return jnp.where(index == 0, lead, jnp.where(index == lead, 0, index))


def keep_kernel(table, out, sem):
    copy = pltpu.make_async_copy(table, out, sem)
    copy.start()
    copy.wait()


def keep(table):
    return pl.pallas_call(
        keep_kernel,
        in_specs=[pl.BlockSpec(memory_space=pltpu.HBM)],
        out_specs=whole(),
        scratch_shapes=[pltpu.SemaphoreType.DMA],
        out_shape=jax.ShapeDtypeStruct(table.shape, table.dtype),
        compiler_params=pltpu.CompilerParams(vmem_limit_bytes=VMEM_BYTES),
        cost_estimate=pl.CostEstimate(flops=0, bytes_accessed=4 * table.size, transcendentals=0),
        name="keep",
    )(table)


def picks_of(sectors, lead, heard, occupied, start_label):
    place = lax.axis_index("site")
    told = heard[:, 0, :]
    earlier = swapped(rows_of(told.shape), lead) < place
    label = jnp.sum(jnp.where(earlier, told, 0), axis=0, keepdims=True) + start_label[...]
    label = label % sectors
    chosen = label + occupied[...] * sectors
    return chosen, label + sectors - occupied[...] * sectors


def fetch_kernel(sectors, lead, heard, occupied, start_label, table, out):
    picks = picks_of(sectors, lead, heard, occupied, start_label)
    for s in range(out.shape[0]):
        for n in range(out.shape[1]):
            out[s, n] = table[picks[n][0, s]].astype(jnp.float32)


def halves(x):
    high = x.astype(jnp.bfloat16)
    return high, (x - high.astype(jnp.float32)).astype(jnp.bfloat16)


def times_exact(left, right):
    rows = left.shape[0]
    both = jnp.dot(
        jnp.concatenate(halves(left), axis=0), right, preferred_element_type=jnp.float32
    )
    return both[:rows] + both[rows:]


def times(left, right):
    high, low = halves(right)
    part = jnp.dot(left.astype(jnp.bfloat16), low, preferred_element_type=jnp.float32)
    return times_exact(left, high) + part


def as_column(row):
    width = row.shape[-1]
    return jnp.broadcast_to(row, (width, width)).T


def row_times(row, block):
    return jnp.sum(as_column(row) * block, axis=0, keepdims=True)


def vectors(blocks, vector, group):
    entering = [vector]
    chosen = [blocks[k, 0].astype(jnp.bfloat16) for k in range(group)]
    for k in range(0, group - 3, 4):
        one, two = (
            jnp.dot(chosen[j], chosen[j + 1], preferred_element_type=jnp.float32)
            for j in (k, k + 2)
        )
        vector = entering[-1]
        middle = row_times(vector, one)
        entering += [
            row_times(vector, blocks[k, 0]),
            middle,
            row_times(middle, blocks[k + 2, 0]),
            row_times(vector, times(one, two)),
        ]
    while len(entering) <= group:
        entering.append(row_times(entering[-1], blocks[len(entering) - 1, 0]))
    return entering


def first_kernel(group, blocks, start, entering, leaving):
    vector = start[pl.ds(lax.axis_index("site") % group, 1), :]
    found = vectors(blocks, vector, group)
    leaving[...] = found[-1]
    for k in range(group):
        entering[k] = found[k]


def products_kernel(group, blocks, product):
    left = blocks[0, 0]
    for k in range(1, group):
        left = times_exact(left, blocks[k, 0].astype(jnp.bfloat16))
    product[...] = left


def shares(of_chosen, of_other, occupied):
    total = of_chosen + of_other + epsilon
    fill = jnp.where(occupied == 1, of_chosen, of_other) / total
    return fill, jnp.log(of_chosen + epsilon) - jnp.log(total)


def squares(row):
    return jnp.sum(row * row, axis=1, keepdims=True)


def site_kernel(sectors, sites, lead, returned, heard, occupied, start_label, table, out):
    place, batch = lax.axis_index("site"), lax.axis_index("batch")
    picks = picks_of(sectors, lead, heard, occupied, start_label)
    samples = returned.shape[0]
    found = [[], []]
    for s in range(samples):
        column = as_column(returned[s])
        for n in range(2):
            block = table[picks[n][0, s]].astype(jnp.float32)
            found[n].append(jnp.sum(column * block, axis=0, keepdims=True))
    of_chosen, of_other = (squares(jnp.concatenate(rows, axis=0)) for rows in found)
    own = (samples, samples)
    mark = jnp.where(lanes_of(own) == rows_of(own), jnp.broadcast_to(occupied[...], own), 0)
    fill, log = shares(of_chosen, of_other, jnp.sum(mark, axis=1, keepdims=True))
    shape = (samples, LANES)
    lane, row = lanes_of(shape), rows_of(shape)
    logs = jnp.sum(jnp.where(lane == row + samples, log, 0.0), axis=0, keepdims=True)
    fills = jnp.sum(jnp.where(lane == row, fill, 0.0), axis=0, keepdims=True)
    cross = jnp.sum(jnp.where(lane == 2 * samples, fill, 0.0), axis=0, keepdims=True)
    to = rows_of(out.shape)
    here, own = to % sites == place, to // sites == batch
    out[...] = jnp.where(own, logs, 0.0) + jnp.where(here, jnp.where(own, fills, cross), 0.0)


def weights_kernel(sites, group, lead, from_site, blocks, arrived, heard, out):
    place, batch = lax.axis_index("site"), lax.axis_index("batch")
    mine, here = place % group, place // group
    groups = sites // group

    @pl.when(here == 0)
    def _():
        out[...] = from_site[...]

    @pl.when(here > 0)
    def _():
        entering = vectors(blocks, arrived[...], group)
        of_chosen = squares(jnp.concatenate(entering[1:], axis=0))
        beside = [row_times(entering[k], blocks[k, 1]) for k in range(group)]
        of_other = squares(jnp.concatenate(beside, axis=0))
        notes = jnp.concatenate(
            [heard[swapped(here * group + k, lead)] for k in range(group)], axis=0
        )
        notes = jnp.where(lanes_of(notes.shape) == mine, notes, 0)
        fill, log = shares(of_chosen, of_other, jnp.sum(notes, axis=1, keepdims=True))
        lane = lanes_of((group, LANES))
        fill_own = jnp.where(lane == mine, fill, 0.0)
        fill_cross = jnp.where(lane == 2 * group, fill, 0.0)
        log_sum = jnp.sum(log, axis=0, keepdims=True)
        logs = jnp.where(lane == group + mine, log_sum, 0.0)
        for b in range(out.shape[0] // sites):
            for g in range(groups):
                at = b * sites + g * group
                fills = jnp.where(batch == b, fill_own, fill_cross)
                out[at : at + group, :] = jnp.where(here == g, fills, 0.0) + jnp.where(
                    batch == b, logs, 0.0
                )


def collect_kernel(sites, batches, reply, fill_probs, mean_logprob, site_fill):
    samples = fill_probs.shape[1]
    row = jnp.sum(reply[...], axis=0, keepdims=True)
    fill_probs[...] = row[:, :samples]
    mean_logprob[...] = row[:, samples : 2 * samples] / sites
    lane = lanes_of(row.shape)
    fills = jnp.where((lane < samples) | (lane == 2 * samples), row, 0.0)
    site_fill[...] = jnp.sum(fills, axis=1, keepdims=True) / (samples * batches)


def call(kernel, out_shape, *arrays, scratch_shapes=(), name=None):
    out_specs = [whole()] * len(out_shape) if isinstance(out_shape, (list, tuple)) else whole()
    return pl.pallas_call(
        kernel,
        in_specs=[whole()] * len(arrays),
        out_specs=out_specs,
        out_shape=out_shape,
        scratch_shapes=scratch_shapes,
        compiler_params=pltpu.CompilerParams(vmem_limit_bytes=VMEM_BYTES),
        name=name,
    )(*arrays)


def on_device(site_tensors, start_vector, start_label, occupations):
    sectors = site_tensors.shape[2]
    width = site_tensors.shape[3]
    sites = lax.axis_size("site")
    batches = lax.axis_size("batch")
    samples = occupations.shape[1]
    group = samples
    groups = sites // group
    everyone = sites * batches
    here = lax.axis_index("site") // group
    f32 = jnp.float32

    table = keep(site_tensors.reshape(2 * sectors, width, width))

    order, lead = first_order(sites)
    told = jnp.broadcast_to(occupations[:, None, :], (sites, 1, samples))
    heard = lax.all_to_all(told, "site", 0, 0, tiled=True, axis_index_groups=[order])

    teams = [[g * group + k for k in range(group)] for g in range(groups)]
    given = (heard, occupations, start_label[None, :], table)
    message_like = jax.ShapeDtypeStruct((everyone, LANES), f32)

    def trade(blocks):
        return lax.all_to_all(blocks, "site", 0, 0, tiled=True, axis_index_groups=teams)

    def fetch(count):
        return call(
            lambda *refs: fetch_kernel(sectors, lead, *refs),
            jax.ShapeDtypeStruct((samples, count, width, width), f32),
            *given,
            name="fetch",
        )

    def first():
        return call(
            lambda *refs: first_kernel(group, *refs),
            (
                jax.ShapeDtypeStruct((group, 1, width), f32),
                jax.ShapeDtypeStruct((1, width), f32),
            ),
            trade(fetch(1)),
            start_vector,
            name="first",
        )

    def first_idle():
        return jnp.zeros((group, 1, width), f32), jnp.zeros((1, width), f32)

    def second(entering):
        message = call(
            lambda *refs: site_kernel(sectors, sites, lead, *refs),
            message_like,
            trade(entering),
            *given,
            name="site_weights",
        )
        return message, jnp.zeros((group, 2, width, width), f32)

    def later(entering):
        return jnp.zeros(message_like.shape, f32), trade(fetch(2))

    entering, leaving = lax.cond(here == 0, first, first_idle)
    vector = leaving
    if groups > 1:
        onward = [(i, i + group) for i in range(group)]
        vector = lax.ppermute(leaving, "site", onward)
    from_site, blocks = lax.cond(here == 0, second, later, entering)
    if groups > 2:
        product = call(
            lambda *refs: products_kernel(group, *refs),
            jax.ShapeDtypeStruct((width, width), f32),
            blocks,
            name="product",
        )
    for turn in range(2, groups):
        leaving = jnp.dot(vector, product, precision=lax.Precision.HIGHEST)
        onward = [(i, i + group) for i in range((turn - 1) * group, turn * group)]
        arrived = lax.ppermute(leaving, "site", onward)
        vector = jnp.where(here == turn, arrived, vector)

    message = call(
        lambda *refs: weights_kernel(sites, group, lead, *refs),
        message_like,
        from_site,
        blocks,
        vector,
        heard,
        name="group_weights",
    )
    reply = lax.all_to_all(message, ("batch", "site"), 0, 0, tiled=True)
    fill_probs, mean_logprob, site_fill = call(
        lambda *refs: collect_kernel(sites, batches, *refs),
        [
            jax.ShapeDtypeStruct((1, samples), f32),
            jax.ShapeDtypeStruct((1, samples), f32),
            jax.ShapeDtypeStruct((1, 1), f32),
        ],
        reply,
        name="collect",
    )
    return (fill_probs, mean_logprob[0], site_fill[0])


def solution(mesh):
    placed = (P("site", None, None, None, None), P("batch", None), P("batch"), P("site", "batch"))
    return jax.shard_map(
        on_device,
        mesh=mesh,
        in_specs=placed,
        out_specs=(P("site", "batch"), P("batch"), P("site")),
        check_vma=False,
    )
```

```python
import jax
import jax.numpy as jnp
from jax import lax
from jax.experimental import pallas as pl
from jax.experimental.pallas import tpu as pltpu
from jax.sharding import PartitionSpec as P

epsilon = 1e-06
LANES = 128
VMEM_BYTES = 24 << 20


def whole():
    return pl.BlockSpec(memory_space=pltpu.VMEM)


def lanes_of(shape):
    return lax.broadcasted_iota(jnp.int32, shape, 1)


def rows_of(shape):
    return lax.broadcasted_iota(jnp.int32, shape, 0)


def led_by(lead, count):
    order = list(range(count))
    order[0], order[lead] = lead, 0
    return order


def swapped(index, lead):
    return jnp.where(index == 0, lead, jnp.where(index == lead, 0, index))


def keep_kernel(table, out, sem):
    copy = pltpu.make_async_copy(table, out, sem)
    copy.start()
    copy.wait()


def keep(table):
    return pl.pallas_call(
        keep_kernel,
        in_specs=[pl.BlockSpec(memory_space=pltpu.HBM)],
        out_specs=whole(),
        scratch_shapes=[pltpu.SemaphoreType.DMA],
        out_shape=jax.ShapeDtypeStruct(table.shape, table.dtype),
        compiler_params=pltpu.CompilerParams(vmem_limit_bytes=VMEM_BYTES),
        cost_estimate=pl.CostEstimate(flops=0, bytes_accessed=4 * table.size, transcendentals=0),
        name="keep",
    )(table)


def picks_of(sectors, lead, heard, occupied, start_label):
    place = lax.axis_index("site")
    told = heard[:, 0, :]
    earlier = swapped(rows_of(told.shape), lead) < place
    label = jnp.sum(jnp.where(earlier, told, 0), axis=0, keepdims=True) + start_label[...]
    label = label % sectors
    chosen = label + occupied[...] * sectors
    return chosen, label + sectors - occupied[...] * sectors


def fetch_kernel(sectors, lead, heard, occupied, start_label, table, out):
    picks = picks_of(sectors, lead, heard, occupied, start_label)
    for s in range(out.shape[0]):
        for n in range(out.shape[1]):
            out[s, n] = table[picks[n][0, s]].astype(jnp.float32)


def times_exact(left, right):
    rows = left.shape[0]
    high = left.astype(jnp.bfloat16)
    low = (left - high.astype(jnp.float32)).astype(jnp.bfloat16)
    both = jnp.dot(
        jnp.concatenate([high, low], axis=0), right, preferred_element_type=jnp.float32
    )
    return both[:rows] + both[rows:]


def as_column(row):
    width = row.shape[-1]
    return jnp.broadcast_to(row, (width, width)).T


def row_times(row, block):
    return jnp.sum(as_column(row) * block, axis=0, keepdims=True)


def vectors(blocks, vector, group):
    entering = [vector]
    pairs = [
        jnp.dot(
            blocks[k, 0].astype(jnp.bfloat16),
            blocks[k + 1, 0].astype(jnp.bfloat16),
            preferred_element_type=jnp.float32,
        )
        for k in range(0, group - 1, 2)
    ]
    for k, pair in zip(range(0, group, 2), pairs):
        vector = entering[-1]
        entering += [row_times(vector, blocks[k, 0]), row_times(vector, pair)]
    if group % 2:
        entering.append(row_times(entering[-1], blocks[group - 1, 0]))
    return entering


def first_kernel(group, back, blocks, start, entering, leaving):
    vector = start[pl.ds(lax.axis_index("site") % group, 1), :]
    found = vectors(blocks, vector, group)
    leaving[...] = found[-1]
    for k in range(group):
        entering[back.index(k)] = found[k]


def products_kernel(group, blocks, product):
    left = blocks[0, 0]
    for k in range(1, group):
        left = times_exact(left, blocks[k, 0].astype(jnp.bfloat16))
    product[...] = left


def shares(of_chosen, of_other, occupied):
    total = of_chosen + of_other + epsilon
    fill = jnp.where(occupied == 1, of_chosen, of_other) / total
    return fill, jnp.log(of_chosen + epsilon) - jnp.log(total)


def squares(row):
    return jnp.sum(row * row, axis=1, keepdims=True)


def site_kernel(sectors, sites, lead, back, returned, heard, occupied, start_label, table, out):
    place, batch = lax.axis_index("site"), lax.axis_index("batch")
    picks = picks_of(sectors, lead, heard, occupied, start_label)
    samples = returned.shape[0]
    found = [[], []]
    for s in range(samples):
        column = as_column(returned[back.index(s)])
        for n in range(2):
            block = table[picks[n][0, s]].astype(jnp.float32)
            found[n].append(jnp.sum(column * block, axis=0, keepdims=True))
    of_chosen, of_other = (squares(jnp.concatenate(rows, axis=0)) for rows in found)
    own = (samples, samples)
    mark = jnp.where(lanes_of(own) == rows_of(own), jnp.broadcast_to(occupied[...], own), 0)
    fill, log = shares(of_chosen, of_other, jnp.sum(mark, axis=1, keepdims=True))
    shape = (samples, LANES)
    lane, row = lanes_of(shape), rows_of(shape)
    logs = jnp.sum(jnp.where(lane == row + samples, log, 0.0), axis=0, keepdims=True)
    fills = jnp.sum(jnp.where(lane == row, fill, 0.0), axis=0, keepdims=True)
    cross = jnp.sum(jnp.where(lane == 2 * samples, fill, 0.0), axis=0, keepdims=True)
    to = rows_of(out.shape)
    here, own = to % sites == place, to // sites == batch
    out[...] = jnp.where(own, logs, 0.0) + jnp.where(here, jnp.where(own, fills, cross), 0.0)


def weights_kernel(sites, group, lead, from_site, blocks, arrived, heard, out):
    place, batch = lax.axis_index("site"), lax.axis_index("batch")
    mine, here = place % group, place // group
    groups = sites // group

    @pl.when(here == 0)
    def _():
        out[...] = from_site[...]

    @pl.when(here > 0)
    def _():
        entering = vectors(blocks, arrived[...], group)
        of_chosen = squares(jnp.concatenate(entering[1:], axis=0))
        beside = [row_times(entering[k], blocks[k, 1]) for k in range(group)]
        of_other = squares(jnp.concatenate(beside, axis=0))
        notes = jnp.concatenate(
            [heard[swapped(here * group + k, lead)] for k in range(group)], axis=0
        )
        notes = jnp.where(lanes_of(notes.shape) == mine, notes, 0)
        fill, log = shares(of_chosen, of_other, jnp.sum(notes, axis=1, keepdims=True))
        lane = lanes_of((group, LANES))
        fill_own = jnp.where(lane == mine, fill, 0.0)
        fill_cross = jnp.where(lane == 2 * group, fill, 0.0)
        log_sum = jnp.sum(log, axis=0, keepdims=True)
        logs = jnp.where(lane == group + mine, log_sum, 0.0)
        for b in range(out.shape[0] // sites):
            for g in range(groups):
                at = b * sites + g * group
                fills = jnp.where(batch == b, fill_own, fill_cross)
                out[at : at + group, :] = jnp.where(here == g, fills, 0.0) + jnp.where(
                    batch == b, logs, 0.0
                )


def collect_kernel(sites, batches, reply, fill_probs, mean_logprob, site_fill):
    samples = fill_probs.shape[1]
    row = jnp.sum(reply[...], axis=0, keepdims=True)
    fill_probs[...] = row[:, :samples]
    mean_logprob[...] = row[:, samples : 2 * samples] / sites
    lane = lanes_of(row.shape)
    fills = jnp.where((lane < samples) | (lane == 2 * samples), row, 0.0)
    site_fill[...] = jnp.sum(fills, axis=1, keepdims=True) / (samples * batches)


def call(kernel, out_shape, *arrays, scratch_shapes=(), name=None):
    out_specs = [whole()] * len(out_shape) if isinstance(out_shape, (list, tuple)) else whole()
    return pl.pallas_call(
        kernel,
        in_specs=[whole()] * len(arrays),
        out_specs=out_specs,
        out_shape=out_shape,
        scratch_shapes=scratch_shapes,
        compiler_params=pltpu.CompilerParams(vmem_limit_bytes=VMEM_BYTES),
        name=name,
    )(*arrays)


def on_device(site_tensors, start_vector, start_label, occupations):
    sectors = site_tensors.shape[2]
    width = site_tensors.shape[3]
    sites = lax.axis_size("site")
    batches = lax.axis_size("batch")
    samples = occupations.shape[1]
    group = samples
    groups = sites // group
    everyone = sites * batches
    here = lax.axis_index("site") // group
    f32 = jnp.float32

    table = keep(site_tensors.reshape(2 * sectors, width, width))

    lead = sites * 3 // 4
    order = led_by(lead, sites)
    told = jnp.broadcast_to(occupations[:, None, :], (sites, 1, samples))
    heard = lax.all_to_all(told, "site", 0, 0, tiled=True, axis_index_groups=[order])

    ahead, back = list(range(group)), led_by(min(2, group - 1), group)
    given = (heard, occupations, start_label[None, :], table)
    message_like = jax.ShapeDtypeStruct((everyone, LANES), f32)

    def trade(parts, order):
        teams = [[g * group + k for k in order] for g in range(groups)]
        return lax.all_to_all(parts, "site", 0, 0, tiled=True, axis_index_groups=teams)

    def fetch(count):
        return call(
            lambda *refs: fetch_kernel(sectors, lead, *refs),
            jax.ShapeDtypeStruct((samples, count, width, width), f32),
            *given,
            name="fetch",
        )

    def first():
        return call(
            lambda *refs: first_kernel(group, back, *refs),
            (
                jax.ShapeDtypeStruct((group, 1, width), f32),
                jax.ShapeDtypeStruct((1, width), f32),
            ),
            trade(fetch(1), ahead),
            start_vector,
            name="first",
        )

    def first_idle():
        return jnp.zeros((group, 1, width), f32), jnp.zeros((1, width), f32)

    def second(entering):
        message = call(
            lambda *refs: site_kernel(sectors, sites, lead, back, *refs),
            message_like,
            trade(entering, back),
            *given,
            name="site_weights",
        )
        return message, jnp.zeros((group, 2, width, width), f32)

    def later(entering):
        return jnp.zeros(message_like.shape, f32), trade(fetch(2), ahead)

    entering, leaving = lax.cond(here == 0, first, first_idle)
    vector = leaving
    if groups > 1:
        onward = [(i, i + group) for i in range(group)]
        vector = lax.ppermute(leaving, "site", onward)
    from_site, blocks = lax.cond(here == 0, second, later, entering)
    if groups > 2:
        product = call(
            lambda *refs: products_kernel(group, *refs),
            jax.ShapeDtypeStruct((width, width), f32),
            blocks,
            name="product",
        )
    for turn in range(2, groups):
        leaving = jnp.dot(vector, product, precision=lax.Precision.HIGHEST)
        onward = [(i, i + group) for i in range((turn - 1) * group, turn * group)]
        arrived = lax.ppermute(leaving, "site", onward)
        vector = jnp.where(here == turn, arrived, vector)

    message = call(
        lambda *refs: weights_kernel(sites, group, lead, *refs),
        message_like,
        from_site,
        blocks,
        vector,
        heard,
        name="group_weights",
    )
    reply = lax.all_to_all(message, ("batch", "site"), 0, 0, tiled=True)
    fill_probs, mean_logprob, site_fill = call(
        lambda *refs: collect_kernel(sites, batches, *refs),
        [
            jax.ShapeDtypeStruct((1, samples), f32),
            jax.ShapeDtypeStruct((1, samples), f32),
            jax.ShapeDtypeStruct((1, 1), f32),
        ],
        reply,
        name="collect",
    )
    return (fill_probs, mean_logprob[0], site_fill[0])


def solution(mesh):
    placed = (P("site", None, None, None, None), P("batch", None), P("batch"), P("site", "batch"))
    return jax.shard_map(
        on_device,
        mesh=mesh,
        in_specs=placed,
        out_specs=(P("site", "batch"), P("batch"), P("site")),
        check_vma=False,
    )
```

```python
import jax
import jax.numpy as jnp
from jax import lax
from jax.experimental import pallas as pl
from jax.experimental.pallas import tpu as pltpu
from jax.sharding import PartitionSpec as P

epsilon = 1e-06
LANES = 128
VMEM_BYTES = 24 << 20


def whole():
    return pl.BlockSpec(memory_space=pltpu.VMEM)


def lanes_of(shape):
    return lax.broadcasted_iota(jnp.int32, shape, 1)


def rows_of(shape):
    return lax.broadcasted_iota(jnp.int32, shape, 0)


def led_by(lead, count):
    order = list(range(count))
    order[0], order[lead] = lead, 0
    return order


def swapped(index, lead):
    return jnp.where(index == 0, lead, jnp.where(index == lead, 0, index))


def keep_kernel(table, out, sem):
    copy = pltpu.make_async_copy(table, out, sem)
    copy.start()
    copy.wait()


def keep(table):
    return pl.pallas_call(
        keep_kernel,
        in_specs=[pl.BlockSpec(memory_space=pltpu.HBM)],
        out_specs=whole(),
        scratch_shapes=[pltpu.SemaphoreType.DMA],
        out_shape=jax.ShapeDtypeStruct(table.shape, table.dtype),
        compiler_params=pltpu.CompilerParams(vmem_limit_bytes=VMEM_BYTES),
        cost_estimate=pl.CostEstimate(flops=0, bytes_accessed=4 * table.size, transcendentals=0),
        name="keep",
    )(table)


def picks_of(sectors, lead, heard, occupied, start_label):
    place = lax.axis_index("site")
    told = heard[:, 0, :]
    earlier = swapped(rows_of(told.shape), lead) < place
    label = jnp.sum(jnp.where(earlier, told, 0), axis=0, keepdims=True) + start_label[...]
    label = label % sectors
    chosen = label + occupied[...] * sectors
    return chosen, label + sectors - occupied[...] * sectors


def fetch_kernel(sectors, lead, heard, occupied, start_label, table, out):
    picks = picks_of(sectors, lead, heard, occupied, start_label)
    for s in range(out.shape[0]):
        for n in range(out.shape[1]):
            out[s, n] = table[picks[n][0, s]].astype(jnp.float32)


def times_exact(left, right):
    rows = left.shape[0]
    high = left.astype(jnp.bfloat16)
    low = (left - high.astype(jnp.float32)).astype(jnp.bfloat16)
    both = jnp.dot(
        jnp.concatenate([high, low], axis=0), right, preferred_element_type=jnp.float32
    )
    return both[:rows] + both[rows:]


def as_column(row):
    width = row.shape[-1]
    return jnp.broadcast_to(row, (width, width)).T


def row_times(row, block):
    return jnp.sum(as_column(row) * block, axis=0, keepdims=True)


def vectors(blocks, vector, group):
    chosen = [blocks[k, 0].astype(jnp.bfloat16) for k in range(group)]
    entering = [vector]
    column = as_column(vector)
    for k in range(0, group - 1, 2):
        entering.append(jnp.sum(column * blocks[k, 0], axis=0, keepdims=True))
        if k % 4 == 0:
            pair = jnp.dot(chosen[k], chosen[k + 1], preferred_element_type=jnp.float32)
            entering.append(jnp.sum(column * pair, axis=0, keepdims=True))
            column = as_column(entering[-1])
        else:
            turned = lax.dot_general(
                chosen[k + 1],
                chosen[k],
                (((0,), (1,)), ((), ())),
                preferred_element_type=jnp.float32,
            )
            after = jnp.sum(turned * entering[-2], axis=1, keepdims=True)
            column = jnp.broadcast_to(after, turned.shape)
            entering.append(column.T[0:1, :])
    if group % 2:
        entering.append(jnp.sum(column * blocks[group - 1, 0], axis=0, keepdims=True))
    return entering


def first_kernel(group, back, blocks, start, entering, leaving):
    vector = start[pl.ds(lax.axis_index("site") % group, 1), :]
    found = vectors(blocks, vector, group)
    leaving[...] = found[-1]
    for k in range(group):
        entering[back.index(k)] = found[k]


def products_kernel(group, blocks, product):
    left = blocks[0, 0]
    for k in range(1, group):
        left = times_exact(left, blocks[k, 0].astype(jnp.bfloat16))
    product[...] = left


def shares(of_chosen, of_other, occupied):
    total = of_chosen + of_other + epsilon
    fill = jnp.where(occupied == 1, of_chosen, of_other) / total
    return fill, jnp.log(of_chosen + epsilon) - jnp.log(total)


def squares(row):
    return jnp.sum(row * row, axis=1, keepdims=True)


def site_kernel(sectors, sites, lead, back, returned, heard, occupied, start_label, table, out):
    place, batch = lax.axis_index("site"), lax.axis_index("batch")
    picks = picks_of(sectors, lead, heard, occupied, start_label)
    samples = returned.shape[0]
    found = [[], []]
    for s in range(samples):
        column = as_column(returned[back.index(s)])
        for n in range(2):
            block = table[picks[n][0, s]].astype(jnp.float32)
            found[n].append(jnp.sum(column * block, axis=0, keepdims=True))
    of_chosen, of_other = (squares(jnp.concatenate(rows, axis=0)) for rows in found)
    own = (samples, samples)
    mark = jnp.where(lanes_of(own) == rows_of(own), jnp.broadcast_to(occupied[...], own), 0)
    fill, log = shares(of_chosen, of_other, jnp.sum(mark, axis=1, keepdims=True))
    shape = (samples, LANES)
    lane, row = lanes_of(shape), rows_of(shape)
    logs = jnp.sum(jnp.where(lane == row + samples, log, 0.0), axis=0, keepdims=True)
    fills = jnp.sum(jnp.where(lane == row, fill, 0.0), axis=0, keepdims=True)
    cross = jnp.sum(jnp.where(lane == 2 * samples, fill, 0.0), axis=0, keepdims=True)
    to = rows_of(out.shape)
    here, own = to % sites == place, to // sites == batch
    out[...] = jnp.where(own, logs, 0.0) + jnp.where(here, jnp.where(own, fills, cross), 0.0)


def weights_kernel(sites, group, lead, from_site, blocks, arrived, heard, out):
    place, batch = lax.axis_index("site"), lax.axis_index("batch")
    mine, here = place % group, place // group
    groups = sites // group

    @pl.when(here == 0)
    def _():
        out[...] = from_site[...]

    @pl.when(here > 0)
    def _():
        entering = vectors(blocks, arrived[...], group)
        of_chosen = squares(jnp.concatenate(entering[1:], axis=0))
        beside = [row_times(entering[k], blocks[k, 1]) for k in range(group)]
        of_other = squares(jnp.concatenate(beside, axis=0))
        notes = jnp.concatenate(
            [heard[swapped(here * group + k, lead)] for k in range(group)], axis=0
        )
        notes = jnp.where(lanes_of(notes.shape) == mine, notes, 0)
        fill, log = shares(of_chosen, of_other, jnp.sum(notes, axis=1, keepdims=True))
        lane = lanes_of((group, LANES))
        fill_own = jnp.where(lane == mine, fill, 0.0)
        fill_cross = jnp.where(lane == 2 * group, fill, 0.0)
        log_sum = jnp.sum(log, axis=0, keepdims=True)
        logs = jnp.where(lane == group + mine, log_sum, 0.0)
        for b in range(out.shape[0] // sites):
            for g in range(groups):
                at = b * sites + g * group
                fills = jnp.where(batch == b, fill_own, fill_cross)
                out[at : at + group, :] = jnp.where(here == g, fills, 0.0) + jnp.where(
                    batch == b, logs, 0.0
                )


def collect_kernel(sites, batches, reply, fill_probs, mean_logprob, site_fill):
    samples = fill_probs.shape[1]
    row = jnp.sum(reply[...], axis=0, keepdims=True)
    fill_probs[...] = row[:, :samples]
    mean_logprob[...] = row[:, samples : 2 * samples] / sites
    lane = lanes_of(row.shape)
    fills = jnp.where((lane < samples) | (lane == 2 * samples), row, 0.0)
    site_fill[...] = jnp.sum(fills, axis=1, keepdims=True) / (samples * batches)


def call(kernel, out_shape, *arrays, scratch_shapes=(), name=None):
    out_specs = [whole()] * len(out_shape) if isinstance(out_shape, (list, tuple)) else whole()
    return pl.pallas_call(
        kernel,
        in_specs=[whole()] * len(arrays),
        out_specs=out_specs,
        out_shape=out_shape,
        scratch_shapes=scratch_shapes,
        compiler_params=pltpu.CompilerParams(vmem_limit_bytes=VMEM_BYTES),
        name=name,
    )(*arrays)


def on_device(site_tensors, start_vector, start_label, occupations):
    sectors = site_tensors.shape[2]
    width = site_tensors.shape[3]
    sites = lax.axis_size("site")
    batches = lax.axis_size("batch")
    samples = occupations.shape[1]
    group = samples
    groups = sites // group
    everyone = sites * batches
    here = lax.axis_index("site") // group
    f32 = jnp.float32

    table = keep(site_tensors.reshape(2 * sectors, width, width))

    lead = sites * 3 // 4
    order = led_by(lead, sites)
    told = jnp.broadcast_to(occupations[:, None, :], (sites, 1, samples))
    heard = lax.all_to_all(told, "site", 0, 0, tiled=True, axis_index_groups=[order])

    ahead, back = list(range(group)), led_by(min(2, group - 1), group)
    given = (heard, occupations, start_label[None, :], table)
    message_like = jax.ShapeDtypeStruct((everyone, LANES), f32)

    def trade(parts, order):
        teams = [[g * group + k for k in order] for g in range(groups)]
        return lax.all_to_all(parts, "site", 0, 0, tiled=True, axis_index_groups=teams)

    def fetch(count):
        return call(
            lambda *refs: fetch_kernel(sectors, lead, *refs),
            jax.ShapeDtypeStruct((samples, count, width, width), f32),
            *given,
            name="fetch",
        )

    def first():
        return call(
            lambda *refs: first_kernel(group, back, *refs),
            (
                jax.ShapeDtypeStruct((group, 1, width), f32),
                jax.ShapeDtypeStruct((1, width), f32),
            ),
            trade(fetch(1), ahead),
            start_vector,
            name="first",
        )

    def first_idle():
        return jnp.zeros((group, 1, width), f32), jnp.zeros((1, width), f32)

    def second(entering):
        message = call(
            lambda *refs: site_kernel(sectors, sites, lead, back, *refs),
            message_like,
            trade(entering, back),
            *given,
            name="site_weights",
        )
        return message, jnp.zeros((group, 2, width, width), f32)

    def later(entering):
        return jnp.zeros(message_like.shape, f32), trade(fetch(2), ahead)

    entering, leaving = lax.cond(here == 0, first, first_idle)
    vector = leaving
    if groups > 1:
        onward = [(i, i + group) for i in range(group)]
        vector = lax.ppermute(leaving, "site", onward)
    from_site, blocks = lax.cond(here == 0, second, later, entering)
    if groups > 2:
        product = call(
            lambda *refs: products_kernel(group, *refs),
            jax.ShapeDtypeStruct((width, width), f32),
            blocks,
            name="product",
        )
    for turn in range(2, groups):
        leaving = jnp.dot(vector, product, precision=lax.Precision.HIGHEST)
        onward = [(i, i + group) for i in range((turn - 1) * group, turn * group)]
        arrived = lax.ppermute(leaving, "site", onward)
        vector = jnp.where(here == turn, arrived, vector)

    message = call(
        lambda *refs: weights_kernel(sites, group, lead, *refs),
        message_like,
        from_site,
        blocks,
        vector,
        heard,
        name="group_weights",
    )
    reply = lax.all_to_all(message, ("batch", "site"), 0, 0, tiled=True)
    fill_probs, mean_logprob, site_fill = call(
        lambda *refs: collect_kernel(sites, batches, *refs),
        [
            jax.ShapeDtypeStruct((1, samples), f32),
            jax.ShapeDtypeStruct((1, samples), f32),
            jax.ShapeDtypeStruct((1, 1), f32),
        ],
        reply,
        name="collect",
    )
    return (fill_probs, mean_logprob[0], site_fill[0])


def solution(mesh):
    placed = (P("site", None, None, None, None), P("batch", None), P("batch"), P("site", "batch"))
    return jax.shard_map(
        on_device,
        mesh=mesh,
        in_specs=placed,
        out_specs=(P("site", "batch"), P("batch"), P("site")),
        check_vma=False,
    )
```

```python
import jax
import jax.numpy as jnp
from jax import lax
from jax.experimental import pallas as pl
from jax.experimental.pallas import tpu as pltpu
from jax.sharding import PartitionSpec as P

epsilon = 1e-06
LANES = 128
VMEM_BYTES = 24 << 20


def whole():
    return pl.BlockSpec(memory_space=pltpu.VMEM)


def lanes_of(shape):
    return lax.broadcasted_iota(jnp.int32, shape, 1)


def rows_of(shape):
    return lax.broadcasted_iota(jnp.int32, shape, 0)


def led_by(lead, count):
    order = list(range(count))
    order[0], order[lead] = lead, 0
    return order


def swapped(index, lead):
    return jnp.where(index == 0, lead, jnp.where(index == lead, 0, index))


def keep_kernel(table, out, sem):
    copy = pltpu.make_async_copy(table, out, sem)
    copy.start()
    copy.wait()


def keep(table):
    return pl.pallas_call(
        keep_kernel,
        in_specs=[pl.BlockSpec(memory_space=pltpu.HBM)],
        out_specs=whole(),
        scratch_shapes=[pltpu.SemaphoreType.DMA],
        out_shape=jax.ShapeDtypeStruct(table.shape, table.dtype),
        compiler_params=pltpu.CompilerParams(vmem_limit_bytes=VMEM_BYTES),
        cost_estimate=pl.CostEstimate(flops=0, bytes_accessed=4 * table.size, transcendentals=0),
        name="keep",
    )(table)


def picks_of(sectors, lead, heard, occupied, start_label):
    place = lax.axis_index("site")
    told = heard[:, 0, :]
    earlier = swapped(rows_of(told.shape), lead) < place
    label = jnp.sum(jnp.where(earlier, told, 0), axis=0, keepdims=True) + start_label[...]
    label = label % sectors
    chosen = label + occupied[...] * sectors
    return chosen, label + sectors - occupied[...] * sectors


def fetch_kernel(sectors, lead, heard, occupied, start_label, table, out, picked):
    picks = picks_of(sectors, lead, heard, occupied, start_label)
    picked[0:1, :], picked[1:2, :] = picks
    for s in range(out.shape[0]):
        for n in range(out.shape[1]):
            out[s, n] = table[picks[n][0, s]].astype(jnp.float32)


def times_exact(left, right):
    rows = left.shape[0]
    high = left.astype(jnp.bfloat16)
    low = (left - high.astype(jnp.float32)).astype(jnp.bfloat16)
    both = jnp.dot(
        jnp.concatenate([high, low], axis=0), right, preferred_element_type=jnp.float32
    )
    return both[:rows] + both[rows:]


def as_column(row):
    width = row.shape[-1]
    return jnp.broadcast_to(row, (width, width)).T


def row_times(row, block):
    return jnp.sum(as_column(row) * block, axis=0, keepdims=True)


def vectors(blocks, vector, group):
    chosen = [blocks[k, 0].astype(jnp.bfloat16) for k in range(group)]
    entering = [vector]
    column = as_column(vector)
    for k in range(0, group - 1, 2):
        entering.append(jnp.sum(column * blocks[k, 0], axis=0, keepdims=True))
        if k % 4 == 0:
            pair = jnp.dot(chosen[k], chosen[k + 1], preferred_element_type=jnp.float32)
            entering.append(jnp.sum(column * pair, axis=0, keepdims=True))
            column = as_column(entering[-1])
        else:
            turned = lax.dot_general(
                chosen[k + 1],
                chosen[k],
                (((0,), (1,)), ((), ())),
                preferred_element_type=jnp.float32,
            )
            after = jnp.sum(turned * entering[-2], axis=1, keepdims=True)
            column = jnp.broadcast_to(after, turned.shape)
            entering.append(column.T[0:1, :])
    if group % 2:
        entering.append(jnp.sum(column * blocks[group - 1, 0], axis=0, keepdims=True))
    return entering


def first_kernel(group, back, blocks, start, entering, leaving):
    vector = start[pl.ds(lax.axis_index("site") % group, 1), :]
    found = vectors(blocks, vector, group)
    leaving[...] = found[-1]
    for k in range(group):
        entering[back.index(k)] = found[k]


def products_kernel(group, blocks, product):
    left = blocks[0, 0]
    for k in range(1, group):
        left = times_exact(left, blocks[k, 0].astype(jnp.bfloat16))
    product[...] = left


def shares(of_chosen, of_other, occupied):
    total = of_chosen + of_other + epsilon
    fill = jnp.where(occupied == 1, of_chosen, of_other) / total
    return fill, jnp.log(of_chosen + epsilon) - jnp.log(total)


def squares(row):
    return jnp.sum(row * row, axis=1, keepdims=True)


def site_kernel(sites, back, returned, picked, occupied, table, out):
    place, batch = lax.axis_index("site"), lax.axis_index("batch")
    picks = [picked[n : n + 1, :] for n in range(2)]
    samples = returned.shape[0]
    found = [[], []]
    for s in range(samples):
        column = as_column(returned[back.index(s)])
        for n in range(2):
            block = table[picks[n][0, s]].astype(jnp.float32)
            found[n].append(jnp.sum(column * block, axis=0, keepdims=True))
    of_chosen, of_other = (squares(jnp.concatenate(rows, axis=0)) for rows in found)
    own = (samples, samples)
    mark = jnp.where(lanes_of(own) == rows_of(own), jnp.broadcast_to(occupied[...], own), 0)
    fill, log = shares(of_chosen, of_other, jnp.sum(mark, axis=1, keepdims=True))
    shape = (samples, LANES)
    lane, row = lanes_of(shape), rows_of(shape)
    logs = jnp.sum(jnp.where(lane == row + samples, log, 0.0), axis=0, keepdims=True)
    fills = jnp.sum(jnp.where(lane == row, fill, 0.0), axis=0, keepdims=True)
    cross = jnp.sum(jnp.where(lane == 2 * samples, fill, 0.0), axis=0, keepdims=True)
    to = rows_of(out.shape)
    here, own = to % sites == place, to // sites == batch
    out[...] = jnp.where(own, logs, 0.0) + jnp.where(here, jnp.where(own, fills, cross), 0.0)


def weights_kernel(sites, group, lead, from_site, blocks, arrived, heard, out):
    place, batch = lax.axis_index("site"), lax.axis_index("batch")
    mine, here = place % group, place // group
    groups = sites // group

    @pl.when(here == 0)
    def _():
        out[...] = from_site[...]

    @pl.when(here > 0)
    def _():
        entering = vectors(blocks, arrived[...], group)
        of_chosen = squares(jnp.concatenate(entering[1:], axis=0))
        beside = [row_times(entering[k], blocks[k, 1]) for k in range(group)]
        of_other = squares(jnp.concatenate(beside, axis=0))
        notes = jnp.concatenate(
            [heard[swapped(here * group + k, lead)] for k in range(group)], axis=0
        )
        notes = jnp.where(lanes_of(notes.shape) == mine, notes, 0)
        fill, log = shares(of_chosen, of_other, jnp.sum(notes, axis=1, keepdims=True))
        lane = lanes_of((group, LANES))
        fill_own = jnp.where(lane == mine, fill, 0.0)
        fill_cross = jnp.where(lane == 2 * group, fill, 0.0)
        log_sum = jnp.sum(log, axis=0, keepdims=True)
        logs = jnp.where(lane == group + mine, log_sum, 0.0)
        for b in range(out.shape[0] // sites):
            for g in range(groups):
                at = b * sites + g * group
                fills = jnp.where(batch == b, fill_own, fill_cross)
                out[at : at + group, :] = jnp.where(here == g, fills, 0.0) + jnp.where(
                    batch == b, logs, 0.0
                )


def collect_kernel(sites, batches, reply, fill_probs, mean_logprob, site_fill):
    samples = fill_probs.shape[1]
    row = jnp.sum(reply[...], axis=0, keepdims=True)
    fill_probs[...] = row[:, :samples]
    mean_logprob[...] = row[:, samples : 2 * samples] / sites
    lane = lanes_of(row.shape)
    fills = jnp.where((lane < samples) | (lane == 2 * samples), row, 0.0)
    site_fill[...] = jnp.sum(fills, axis=1, keepdims=True) / (samples * batches)


def call(kernel, out_shape, *arrays, scratch_shapes=(), name=None):
    out_specs = [whole()] * len(out_shape) if isinstance(out_shape, (list, tuple)) else whole()
    return pl.pallas_call(
        kernel,
        in_specs=[whole()] * len(arrays),
        out_specs=out_specs,
        out_shape=out_shape,
        scratch_shapes=scratch_shapes,
        compiler_params=pltpu.CompilerParams(vmem_limit_bytes=VMEM_BYTES),
        name=name,
    )(*arrays)


def on_device(site_tensors, start_vector, start_label, occupations):
    sectors = site_tensors.shape[2]
    width = site_tensors.shape[3]
    sites = lax.axis_size("site")
    batches = lax.axis_size("batch")
    samples = occupations.shape[1]
    group = samples
    groups = sites // group
    everyone = sites * batches
    here = lax.axis_index("site") // group
    f32 = jnp.float32

    table = keep(site_tensors.reshape(2 * sectors, width, width))

    lead = sites * 3 // 4
    order = led_by(lead, sites)
    told = jnp.broadcast_to(occupations[:, None, :], (sites, 1, samples))
    heard = lax.all_to_all(told, "site", 0, 0, tiled=True, axis_index_groups=[order])

    ahead, back = list(range(group)), led_by(min(2, group - 1), group)
    given = (heard, occupations, start_label[None, :], table)
    message_like = jax.ShapeDtypeStruct((everyone, LANES), f32)

    def trade(parts, order):
        teams = [[g * group + k for k in order] for g in range(groups)]
        return lax.all_to_all(parts, "site", 0, 0, tiled=True, axis_index_groups=teams)

    def fetch(count):
        return call(
            lambda *refs: fetch_kernel(sectors, lead, *refs),
            (
                jax.ShapeDtypeStruct((samples, count, width, width), f32),
                jax.ShapeDtypeStruct((2, samples), jnp.int32),
            ),
            *given,
            name="fetch",
        )

    def first():
        blocks, picked = fetch(1)
        entering, leaving = call(
            lambda *refs: first_kernel(group, back, *refs),
            (
                jax.ShapeDtypeStruct((group, 1, width), f32),
                jax.ShapeDtypeStruct((1, width), f32),
            ),
            trade(blocks, ahead),
            start_vector,
            name="first",
        )
        return entering, leaving, picked

    def first_idle():
        return (
            jnp.zeros((group, 1, width), f32),
            jnp.zeros((1, width), f32),
            jnp.zeros((2, samples), jnp.int32),
        )

    def second(entering, picked):
        message = call(
            lambda *refs: site_kernel(sites, back, *refs),
            message_like,
            trade(entering, back),
            picked,
            occupations,
            table,
            name="site_weights",
        )
        return message, jnp.zeros((group, 2, width, width), f32)

    def later(entering, picked):
        return jnp.zeros(message_like.shape, f32), trade(fetch(2)[0], ahead)

    entering, leaving, picked = lax.cond(here == 0, first, first_idle)
    vector = leaving
    if groups > 1:
        onward = [(i, i + group) for i in range(group)]
        vector = lax.ppermute(leaving, "site", onward)
    from_site, blocks = lax.cond(here == 0, second, later, entering, picked)
    if groups > 2:
        product = call(
            lambda *refs: products_kernel(group, *refs),
            jax.ShapeDtypeStruct((width, width), f32),
            blocks,
            name="product",
        )
    for turn in range(2, groups):
        leaving = jnp.dot(vector, product, precision=lax.Precision.HIGHEST)
        onward = [(i, i + group) for i in range((turn - 1) * group, turn * group)]
        arrived = lax.ppermute(leaving, "site", onward)
        vector = jnp.where(here == turn, arrived, vector)

    message = call(
        lambda *refs: weights_kernel(sites, group, lead, *refs),
        message_like,
        from_site,
        blocks,
        vector,
        heard,
        name="group_weights",
    )
    reply = lax.all_to_all(message, ("batch", "site"), 0, 0, tiled=True)
    fill_probs, mean_logprob, site_fill = call(
        lambda *refs: collect_kernel(sites, batches, *refs),
        [
            jax.ShapeDtypeStruct((1, samples), f32),
            jax.ShapeDtypeStruct((1, samples), f32),
            jax.ShapeDtypeStruct((1, 1), f32),
        ],
        reply,
        name="collect",
    )
    return (fill_probs, mean_logprob[0], site_fill[0])


def solution(mesh):
    placed = (P("site", None, None, None, None), P("batch", None), P("batch"), P("site", "batch"))
    return jax.shard_map(
        on_device,
        mesh=mesh,
        in_specs=placed,
        out_specs=(P("site", "batch"), P("batch"), P("site")),
        check_vma=False,
    )
```

```python
import jax
import jax.numpy as jnp
from jax import lax
from jax.experimental import pallas as pl
from jax.experimental.pallas import tpu as pltpu
from jax.sharding import PartitionSpec as P

epsilon = 1e-06
LANES = 128
VMEM_BYTES = 24 << 20


def whole():
    return pl.BlockSpec(memory_space=pltpu.VMEM)


def lanes_of(shape):
    return lax.broadcasted_iota(jnp.int32, shape, 1)


def rows_of(shape):
    return lax.broadcasted_iota(jnp.int32, shape, 0)


def led_by(lead, count):
    order = list(range(count))
    order[0], order[lead] = lead, 0
    return order


def swapped(index, lead):
    return jnp.where(index == 0, lead, jnp.where(index == lead, 0, index))


def keep_kernel(table, out, sem):
    copy = pltpu.make_async_copy(table, out, sem)
    copy.start()
    copy.wait()


def keep(table):
    return pl.pallas_call(
        keep_kernel,
        in_specs=[pl.BlockSpec(memory_space=pltpu.HBM)],
        out_specs=whole(),
        scratch_shapes=[pltpu.SemaphoreType.DMA],
        out_shape=jax.ShapeDtypeStruct(table.shape, table.dtype),
        compiler_params=pltpu.CompilerParams(vmem_limit_bytes=VMEM_BYTES),
        cost_estimate=pl.CostEstimate(flops=0, bytes_accessed=4 * table.size, transcendentals=0),
        name="keep",
    )(table)


def picks_of(sectors, lead, heard, occupied, start_label):
    place = lax.axis_index("site")
    told = heard[:, 0, :]
    earlier = swapped(rows_of(told.shape), lead) < place
    label = jnp.sum(jnp.where(earlier, told, 0), axis=0, keepdims=True) + start_label[...]
    label = label % sectors
    chosen = label + occupied[...] * sectors
    return chosen, label + sectors - occupied[...] * sectors


def fetch_kernel(sectors, lead, heard, occupied, start_label, table, out, picked):
    picks = picks_of(sectors, lead, heard, occupied, start_label)
    picked[0:1, :], picked[1:2, :] = picks
    for s in range(out.shape[0]):
        for n in range(out.shape[1]):
            out[s, n] = table[picks[n][0, s]].astype(jnp.float32)


def times_exact(left, right):
    rows = left.shape[0]
    high = left.astype(jnp.bfloat16)
    low = (left - high.astype(jnp.float32)).astype(jnp.bfloat16)
    both = jnp.dot(
        jnp.concatenate([high, low], axis=0), right, preferred_element_type=jnp.float32
    )
    return both[:rows] + both[rows:]


def as_column(row):
    width = row.shape[-1]
    return jnp.broadcast_to(row, (width, width)).T


def row_times(row, block):
    return jnp.sum(as_column(row) * block, axis=0, keepdims=True)


def vectors(blocks, vector, group):
    chosen = [blocks[k, 0].astype(jnp.bfloat16) for k in range(group)]
    entering = [vector]
    column = as_column(vector)
    for k in range(0, group - 1, 2):
        entering.append(jnp.sum(column * blocks[k, 0], axis=0, keepdims=True))
        if k % 4 == 0:
            pair = jnp.dot(chosen[k], chosen[k + 1], preferred_element_type=jnp.float32)
            entering.append(jnp.sum(column * pair, axis=0, keepdims=True))
            column = as_column(entering[-1])
        else:
            turned = lax.dot_general(
                chosen[k + 1],
                chosen[k],
                (((0,), (1,)), ((), ())),
                preferred_element_type=jnp.float32,
            )
            after = jnp.sum(turned * entering[-2], axis=1, keepdims=True)
            column = jnp.broadcast_to(after, turned.shape)
            entering.append(column.T[0:1, :])
    if group % 2:
        entering.append(jnp.sum(column * blocks[group - 1, 0], axis=0, keepdims=True))
    return entering


def first_kernel(group, back, blocks, start, entering, leaving):
    vector = start[pl.ds(lax.axis_index("site") % group, 1), :]
    found = vectors(blocks, vector, group)
    leaving[...] = found[-1]
    for k in range(group):
        entering[back.index(k)] = found[k]


def products_kernel(group, blocks, product):
    left = blocks[0, 0]
    for k in range(1, group):
        left = times_exact(left, blocks[k, 0].astype(jnp.bfloat16))
    product[...] = left


def shares(of_chosen, of_other, occupied):
    total = of_chosen + of_other + epsilon
    fill = jnp.where(occupied == 1, of_chosen, of_other) / total
    return fill, jnp.log(of_chosen + epsilon) - jnp.log(total)


def squares(row):
    return jnp.sum(row * row, axis=1, keepdims=True)


def site_kernel(sites, back, returned, picked, occupied, table, out):
    place, batch = lax.axis_index("site"), lax.axis_index("batch")
    picks = [picked[n : n + 1, :] for n in range(2)]
    samples = returned.shape[0]
    found = [[], []]
    for s in range(samples):
        column = as_column(returned[back.index(s)])
        for n in range(2):
            block = table[picks[n][0, s]].astype(jnp.float32)
            found[n].append(jnp.sum(column * block, axis=0, keepdims=True))
    of_chosen, of_other = (squares(jnp.concatenate(rows, axis=0)) for rows in found)
    own = (samples, samples)
    mark = jnp.where(lanes_of(own) == rows_of(own), jnp.broadcast_to(occupied[...], own), 0)
    fill, log = shares(of_chosen, of_other, jnp.sum(mark, axis=1, keepdims=True))
    shape = (samples, LANES)
    lane, row = lanes_of(shape), rows_of(shape)
    logs = jnp.sum(jnp.where(lane == row + samples, log, 0.0), axis=0, keepdims=True)
    fills = jnp.sum(jnp.where(lane == row, fill, 0.0), axis=0, keepdims=True)
    cross = jnp.sum(jnp.where(lane == 2 * samples, fill, 0.0), axis=0, keepdims=True)
    to = rows_of(out.shape)
    here, own = to % sites == place, to // sites == batch
    out[...] = jnp.where(own, logs, 0.0) + jnp.where(here, jnp.where(own, fills, cross), 0.0)


def weights_kernel(sites, group, lead, from_site, blocks, arrived, heard, out):
    place, batch = lax.axis_index("site"), lax.axis_index("batch")
    mine, here = place % group, place // group
    groups = sites // group

    @pl.when(here == 0)
    def _():
        out[...] = from_site[...]

    @pl.when(here > 0)
    def _():
        entering = vectors(blocks, arrived[...], group)
        of_chosen = squares(jnp.concatenate(entering[1:], axis=0))
        beside = [row_times(entering[k], blocks[k, 1]) for k in range(group)]
        of_other = squares(jnp.concatenate(beside, axis=0))
        notes = jnp.concatenate(
            [heard[swapped(here * group + k, lead)] for k in range(group)], axis=0
        )
        notes = jnp.where(lanes_of(notes.shape) == mine, notes, 0)
        fill, log = shares(of_chosen, of_other, jnp.sum(notes, axis=1, keepdims=True))
        lane = lanes_of((group, LANES))
        fill_own = jnp.where(lane == mine, fill, 0.0)
        fill_cross = jnp.where(lane == 2 * group, fill, 0.0)
        log_sum = jnp.sum(log, axis=0, keepdims=True)
        logs = jnp.where(lane == group + mine, log_sum, 0.0)
        for b in range(out.shape[0] // sites):
            for g in range(groups):
                at = b * sites + g * group
                fills = jnp.where(batch == b, fill_own, fill_cross)
                out[at : at + group, :] = jnp.where(here == g, fills, 0.0) + jnp.where(
                    batch == b, logs, 0.0
                )


def collect_kernel(sites, batches, reply, fill_probs, mean_logprob, site_fill):
    samples = fill_probs.shape[1]
    row = jnp.sum(reply[...], axis=0, keepdims=True)
    fill_probs[...] = row[:, :samples]
    mean_logprob[...] = row[:, samples : 2 * samples] / sites
    lane = lanes_of(row.shape)
    fills = jnp.where((lane < samples) | (lane == 2 * samples), row, 0.0)
    site_fill[...] = jnp.sum(fills, axis=1, keepdims=True) / (samples * batches)


def call(kernel, out_shape, *arrays, scratch_shapes=(), name=None):
    out_specs = [whole()] * len(out_shape) if isinstance(out_shape, (list, tuple)) else whole()
    return pl.pallas_call(
        kernel,
        in_specs=[whole()] * len(arrays),
        out_specs=out_specs,
        out_shape=out_shape,
        scratch_shapes=scratch_shapes,
        compiler_params=pltpu.CompilerParams(vmem_limit_bytes=VMEM_BYTES),
        name=name,
    )(*arrays)


def on_device(site_tensors, start_vector, start_label, occupations):
    sectors = site_tensors.shape[2]
    width = site_tensors.shape[3]
    sites = lax.axis_size("site")
    batches = lax.axis_size("batch")
    samples = occupations.shape[1]
    group = samples
    groups = sites // group
    everyone = sites * batches
    here = lax.axis_index("site") // group
    f32 = jnp.float32

    table = keep(site_tensors.reshape(2 * sectors, width, width))

    lead = sites * 9 // 16
    order = led_by(lead, sites)
    told = jnp.broadcast_to(occupations[:, None, :], (sites, 1, samples))
    heard = lax.all_to_all(told, "site", 0, 0, tiled=True, axis_index_groups=[order])

    ahead, back = list(range(group)), led_by(min(2, group - 1), group)
    given = (heard, occupations, start_label[None, :], table)
    message_like = jax.ShapeDtypeStruct((everyone, LANES), f32)

    def trade(parts, order):
        teams = [[g * group + k for k in order] for g in range(groups)]
        return lax.all_to_all(parts, "site", 0, 0, tiled=True, axis_index_groups=teams)

    def fetch(count):
        return call(
            lambda *refs: fetch_kernel(sectors, lead, *refs),
            (
                jax.ShapeDtypeStruct((samples, count, width, width), f32),
                jax.ShapeDtypeStruct((2, samples), jnp.int32),
            ),
            *given,
            name="fetch",
        )

    def first():
        blocks, picked = fetch(1)
        entering, leaving = call(
            lambda *refs: first_kernel(group, back, *refs),
            (
                jax.ShapeDtypeStruct((group, 1, width), f32),
                jax.ShapeDtypeStruct((1, width), f32),
            ),
            trade(blocks, ahead),
            start_vector,
            name="first",
        )
        return entering, leaving, picked

    def first_idle():
        return (
            jnp.zeros((group, 1, width), f32),
            jnp.zeros((1, width), f32),
            jnp.zeros((2, samples), jnp.int32),
        )

    def second(entering, picked):
        message = call(
            lambda *refs: site_kernel(sites, back, *refs),
            message_like,
            trade(entering, back),
            picked,
            occupations,
            table,
            name="site_weights",
        )
        return message, jnp.zeros((group, 2, width, width), f32)

    def later(entering, picked):
        return jnp.zeros(message_like.shape, f32), trade(fetch(2)[0], ahead)

    entering, leaving, picked = lax.cond(here == 0, first, first_idle)
    vector = leaving
    if groups > 1:
        onward = [(i, i + group) for i in range(group)]
        vector = lax.ppermute(leaving, "site", onward)
    from_site, blocks = lax.cond(here == 0, second, later, entering, picked)
    if groups > 2:
        product = call(
            lambda *refs: products_kernel(group, *refs),
            jax.ShapeDtypeStruct((width, width), f32),
            blocks,
            name="product",
        )
    for turn in range(2, groups):
        leaving = jnp.dot(vector, product, precision=lax.Precision.HIGHEST)
        onward = [(i, i + group) for i in range((turn - 1) * group, turn * group)]
        arrived = lax.ppermute(leaving, "site", onward)
        vector = jnp.where(here == turn, arrived, vector)

    message = call(
        lambda *refs: weights_kernel(sites, group, lead, *refs),
        message_like,
        from_site,
        blocks,
        vector,
        heard,
        name="group_weights",
    )
    reply = lax.all_to_all(message, ("batch", "site"), 0, 0, tiled=True)
    fill_probs, mean_logprob, site_fill = call(
        lambda *refs: collect_kernel(sites, batches, *refs),
        [
            jax.ShapeDtypeStruct((1, samples), f32),
            jax.ShapeDtypeStruct((1, samples), f32),
            jax.ShapeDtypeStruct((1, 1), f32),
        ],
        reply,
        name="collect",
    )
    return (fill_probs, mean_logprob[0], site_fill[0])


def solution(mesh):
    placed = (P("site", None, None, None, None), P("batch", None), P("batch"), P("site", "batch"))
    return jax.shard_map(
        on_device,
        mesh=mesh,
        in_specs=placed,
        out_specs=(P("site", "batch"), P("batch"), P("site")),
        check_vma=False,
    )
```
